32 devices in a mesh: expert: 16 (over z, y, core), dp: 2 (over x).
Axes of the slice: x: 2, y: 2, z: 4, core: 2. Of those that a mesh axis runs over, the one named last changes fastest.
Arguments:
- tokens: bfloat16 [4096, 2048], P(('dp', 'expert')), parts along dimension 0, may hold values from -6 to 6
- expert_ids: int32 [4096, 8], P(('dp', 'expert')), parts along dimension 0, may hold values from 0 to 15, all different within a row; in each aligned block of 128 rows (0 to 127, 128 to 255, ...) at most 72 rows name the same one
- route_weight: float32 [4096, 8], P(('dp', 'expert')), parts along dimension 0, may hold values from 0.05 to 1
- w_gate: bfloat16 [16, 2, 2048, 384], P('expert'), may hold values from -0.125 to 0.125
- w_up: bfloat16 [16, 2, 2048, 384], P('expert'), may hold values from -0.125 to 0.125
- w_down: bfloat16 [16, 2, 384, 2048], P('expert'), may hold values from -0.21875 to 0.21875
Outputs:
- mixed: bfloat16 [4096, 2048], P(('dp', 'expert')), parts along dimension 0
The draws below stay inside these ranges and needn't reach their ends.
There are 2 independent parts, one for each index of `dp`. The reference program is written for one: setup_inputs(seed, part) draws one part's arguments, and reference() takes and returns one part's arrays. A program takes and returns all parts, laid end to end along the dimension named above; an argument that names none is the same for every part. Nothing has to cross between parts.
Inputs may be any that keep to these rules, and one draw needn't show every extreme that they name: `expert_ids`: each row names 8 different experts. In the rows of one device (aligned blocks of 128 rows) no expert is named by more than 72 rows, a bound that some block reaches.
All inputs are finite; a program needn't handle non-finite values.
Results may differ from the reference program's by a relative error of at most 0.0071.
Values may be sent and summed in bfloat16 or wider, within the bound.
A program may use at most 128 MiB of HBM per device.

```python
import math
import jax
import jax.numpy as jnp
import numpy as np
from jax import lax

D = 2048
HID = 768
TOPK = 8
TOK_DEV = 128
HALF = 384
EXPERTS = 16
CAP = 72
TOKENS = 2048
N_EXPERT = 16


def steps_of(key, shape, pieces, low, top_value):
    factor_of = 1.0
    for dim, parts in pieces:
        steps = jax.random.uniform(jax.random.fold_in(jax.random.fold_in(key, 6), dim), (parts,), jnp.float32, low / len(pieces), top_value / len(pieces))
        factor_of = factor_of * jnp.repeat(jnp.exp(steps), shape[dim] // parts).reshape((-1,) + (1,) * (len(shape) - 1 - dim))
    return factor_of


def shared_out(rng, own, number, rows, amount, top, most, skew):
    sequence = jax.random.permutation(rng, amount)
    packed, common = load_shares(amount, rows * top, most, skew, True), load_shares(amount, rows * top, most, skew, False)
    places = jnp.arange(amount)

    def named(lengths, turn):
        used = int((lengths > 0).sum())
        fixed = max(1, used // 4)
        shifted = fixed + (places - fixed + turn * (used - fixed)) % max(1, amount - fixed)
        return jnp.zeros((amount,), jnp.int32).at[sequence[jnp.where(places < fixed, places, shifted)]].set(jnp.asarray(lengths, jnp.int32))

    lengths = jnp.where(number % 4 == 0, named(packed, number // 4), named(common, number - number // 4 - 1))
    mixed = jax.random.permutation(jax.random.fold_in(own, 3), amount)
    donor, taker = mixed[0:amount // 2 * 2:2], mixed[1:amount // 2 * 2:2]
    slack = jnp.minimum(lengths[donor] - 1, most - lengths[taker]) // 2
    slack = jnp.where((donor == sequence[0]) | (taker == sequence[0]) | (lengths[taker] == 0), 0, jnp.maximum(slack, 0))
    shifted = jax.random.randint(jax.random.fold_in(own, 4), (amount // 2,), 0, 1 << 20) % (slack + 1)
    lengths = lengths.at[donor].add(-shifted).at[taker].add(shifted)
    items = jnp.searchsorted(jnp.cumsum(lengths), jnp.arange(rows * top), side="right").astype(jnp.int32)
    listing = items.reshape(top, rows).T
    listing = listing[jax.random.permutation(jax.random.fold_in(own, 1), rows)]
    turn = jax.random.randint(jax.random.fold_in(own, 2), (rows, 1), 0, top)
    return jnp.take_along_axis(listing, (jnp.arange(top)[None, :] + turn) % top, axis=1)


def load_shares(amount, total, bound, lean, full):
    weights = [(1 << 20) // math.isqrt(grade ** lean) + 1 for grade in range(1, amount + 1)]
    largest = bound if full else min(bound, max(-(-total // amount), total * weights[0] // sum(weights)))
    least = 1 if total - largest >= amount - 1 else 0
    given, surplus = [largest] + [least] * (amount - 1), total - largest - least * (amount - 1)
    while surplus > 0:
        candidates = [i for i in range(1, amount) if given[i] < largest] or [i for i in range(1, amount) if given[i] < bound]
        whole, left = sum([weights[i] for i in candidates]), surplus
        for i in candidates:
            extra = min(bound - given[i], max(1, left * weights[i] // whole), surplus)
            given[i] = given[i] + extra
            surplus = surplus - extra
    return np.array(given)


def scatter_about(key, dims, width, reach, split=(), held_as=jnp.bfloat16):
    drawn = width * jax.random.normal(key, dims, jnp.float32)
    if split:
        drawn = drawn * steps_of(key, dims, split, -0.22, 0.18)
    return jnp.clip(drawn, -reach, reach).astype(held_as)


def setup_inputs(seed: int = 0, part: int = 0) -> dict:
    arg_keys = jax.random.split(jax.random.key(seed), 7)
    part_keys = jax.random.split(jax.random.fold_in(arg_keys[6], part), 7)
    tokens = scatter_about(part_keys[0], (TOKENS, D), 1.0, 6.0, ((0, 16),))
    expert_ids_keys = jax.random.split(jax.random.fold_in(part_keys[1], 1), TOKENS // TOK_DEV)
    expert_ids_turns = jax.random.permutation(jax.random.fold_in(part_keys[1], 3), TOKENS // TOK_DEV)
    expert_ids = jax.vmap(lambda own, number: shared_out(jax.random.fold_in(part_keys[1], 2), own, number, TOK_DEV, EXPERTS, TOPK, CAP, 1))(expert_ids_keys, expert_ids_turns).reshape((TOKENS, TOPK))
    route_weight = jnp.clip(jnp.exp(math.log(1.0) - 2.9957323 * jax.random.uniform(part_keys[2], (TOKENS, TOPK), jnp.float32) ** steps_of(part_keys[2], (TOKENS, TOPK), ((0, 16),), -0.2, 0.2)), 0.05, 1.0)
    w_gate = scatter_about(arg_keys[3], (EXPERTS, 2, D, HALF), D ** -0.5, 0.125, ((0, 16),))
    w_up = scatter_about(arg_keys[4], (EXPERTS, 2, D, HALF), D ** -0.5, 0.125, ((0, 16),))
    w_down = scatter_about(arg_keys[5], (EXPERTS, 2, HALF, D), HID ** -0.5, 0.21875, ((0, 16),))
    return dict(tokens=tokens, expert_ids=expert_ids, route_weight=route_weight, w_gate=w_gate, w_up=w_up, w_down=w_down)


def reference(tokens, expert_ids, route_weight, w_gate, w_up, w_down):
    gates = (route_weight / jnp.sum(route_weight, axis=1, keepdims=True)).astype(jnp.bfloat16)
    block_ids = expert_ids.reshape(N_EXPERT, TOK_DEV * TOPK)
    onehot = (block_ids[:, :, None] == jnp.arange(EXPERTS, dtype=jnp.int32)[None, None, :]).astype(jnp.int32)
    before = jnp.cumsum(onehot, axis=1) - onehot
    slot = jnp.sum(before * onehot, axis=2)
    source = jnp.arange(N_EXPERT, dtype=jnp.int32)[:, None]
    per_expert = N_EXPERT * CAP
    position = (block_ids * per_expert + source * CAP + slot).reshape(-1).astype(jnp.int32)
    token_index = (jnp.arange(TOKENS * TOPK, dtype=jnp.int32) // TOPK).astype(jnp.int32)
    table_tok = jnp.zeros((EXPERTS * per_expert,), jnp.int32).at[position].set(token_index)
    table_live = jnp.zeros((EXPERTS * per_expert,), jnp.bfloat16).at[position].set(jnp.ones((TOKENS * TOPK,), jnp.bfloat16))
    table_gate = jnp.zeros((EXPERTS * per_expert,), jnp.bfloat16).at[position].set(gates.reshape(-1))
    table_tok = table_tok.reshape(EXPERTS, per_expert)
    table_live = table_live.reshape(EXPERTS, per_expert)
    table_gate = table_gate.reshape(EXPERTS, per_expert)
    gate_pairs = w_gate.reshape(EXPERTS // 2, 2, 2, D, HALF)
    up_pairs = w_up.reshape(EXPERTS // 2, 2, 2, D, HALF)
    down_pairs = w_down.reshape(EXPERTS // 2, 2, 2, HALF, D)

    def one_expert(expert):
        pair = expert // 2
        inner = expert % 2
        rows = tokens[table_tok[expert]] * table_live[expert][:, None]
        weight_g = table_gate[expert].astype(jnp.float32)[:, None]
        partials = []
        for half in range(2):
            wg = gate_pairs[pair, half, inner]
            wu = up_pairs[pair, half, inner]
            wd = down_pairs[pair, half, inner]
            gate_h = jnp.dot(rows, wg, preferred_element_type=jnp.float32)
            up_h = jnp.dot(rows, wu, preferred_element_type=jnp.float32)
            hidden = (jax.nn.silu(gate_h) * up_h).astype(jnp.bfloat16)
            partial_value = (jnp.dot(hidden, wd, preferred_element_type=jnp.float32) * weight_g).astype(jnp.bfloat16)
            partials.append(partial_value)
        return (partials[0].astype(jnp.float32) + partials[1].astype(jnp.float32)).astype(jnp.bfloat16)

    combined = lax.map(one_expert, jnp.arange(EXPERTS, dtype=jnp.int32))
    flat = combined.reshape(EXPERTS * per_expert, D)
    picked = flat[position].reshape(TOKENS, TOPK, D)
    return jnp.sum(picked.astype(jnp.float32), axis=1).astype(jnp.bfloat16)
```

```python
import functools

import jax
import jax.numpy as jnp
from jax import lax
from jax.experimental import pallas as pl
from jax.experimental.pallas import tpu as pltpu
from jax.sharding import PartitionSpec as P


def chip_cycle(chips_n, rows_n):
    if rows_n % 2 or chips_n % rows_n or chips_n // rows_n < 2:
        return list(range(chips_n))
    deep = chips_n // rows_n
    walk = []
    for y in range(rows_n):
        zs = range(1, deep) if y % 2 == 0 else range(deep - 1, 0, -1)
        walk += [z * rows_n + y for z in zs]
    return walk + list(range(rows_n - 1, -1, -1))


def ffn_kernel(x_ref, gate_ref, g0, u0, d0, g1, u1, d1, out_ref):
    i = pl.program_id(0)
    x = x_ref[...]
    weight = jnp.where(i % 2 == 0, gate_ref[:, 0:1], gate_ref[:, 1:2])

    def add(g_ref, u_ref, d_ref, first):
        gate_h = jnp.dot(x, g_ref[0], preferred_element_type=jnp.float32)
        up_h = jnp.dot(x, u_ref[0], preferred_element_type=jnp.float32)
        hidden = gate_h / (1.0 + jnp.exp(-gate_h)) * up_h
        hidden = hidden.astype(jnp.bfloat16)
        part = jnp.dot(hidden, d_ref[0], preferred_element_type=jnp.float32) * weight

        if first:

            @pl.when(i == 0)
            def _():
                out_ref[...] = part

            @pl.when(i > 0)
            def _():
                out_ref[...] += part

        else:
            out_ref[...] += part

    @pl.when(i < 2)
    def _():
        add(g0, u0, d0, True)

    @pl.when(i >= 2)
    def _():
        add(g1, u1, d1, False)


def ffn(x, gates, own, other):
    rows, width = x.shape
    half = own[0].shape[2]

    def early(shape):
        return pl.BlockSpec((1,) + shape, lambda i: (jnp.minimum(i, 1), 0, 0))

    def late(shape):
        return pl.BlockSpec((1,) + shape, lambda i: (jnp.maximum(i - 2, 0), 0, 0))

    flops = 4 * 2 * 3 * rows * width * half
    moved = 4 * 3 * width * half * 2 + rows * width * 6
    return pl.pallas_call(
        ffn_kernel,
        grid=(4,),
        out_shape=jax.ShapeDtypeStruct((rows, width), jnp.float32),
        in_specs=[
            pl.BlockSpec((rows, width), lambda i: (0, 0)),
            pl.BlockSpec((rows, 2), lambda i: (0, 0)),
            early((width, half)),
            early((width, half)),
            early((half, width)),
            late((width, half)),
            late((width, half)),
            late((half, width)),
        ],
        out_specs=pl.BlockSpec((rows, width), lambda i: (0, 0)),
        cost_estimate=pl.CostEstimate(
            flops=flops, bytes_accessed=moved, transcendentals=4 * rows * half
        ),
        compiler_params=pltpu.CompilerParams(vmem_limit_bytes=48 * 2**20),
    )(x, gates, *own, *other)


def on_device(cycle, tokens, expert_ids, route_weight, w_gate, w_up, w_down):
    devices_n = lax.axis_size("expert")
    index = lax.axis_index("expert")
    chips_n = devices_n // 2
    chip, core = index // 2, index % 2
    rows = tokens.shape[0]
    cut = rows // 2
    far = chips_n // 2
    place = [0] * chips_n
    for i, c in enumerate(cycle):
        place[c] = i

    def turn(step):
        pairs = []
        for i, c in enumerate(cycle):
            to = cycle[(i + step) % chips_n]
            pairs += [(2 * c, 2 * to), (2 * c + 1, 2 * to + 1)]
        return pairs

    right, left = turn(1), turn(-1)
    swap = [(i, i ^ 1) for i in range(devices_n)]
    send = lambda value, pairs: lax.ppermute(value, "expert", pairs)

    gates = (route_weight / jnp.sum(route_weight, axis=1, keepdims=True)).astype(jnp.bfloat16)
    chosen = expert_ids[:, :, None] == jnp.arange(devices_n, dtype=jnp.int32)
    dense = jnp.sum(jnp.where(chosen, gates.astype(jnp.float32)[:, :, None], 0.0), axis=1)

    own = (w_gate[0], w_up[0], w_down[0])
    other = tuple(send(w, swap) for w in own)
    all_gates = lax.all_gather(dense.astype(jnp.bfloat16), "expert")
    all_gates = all_gates.reshape(chips_n, 2, rows, devices_n)
    all_gates = lax.dynamic_index_in_dim(all_gates, core, 1, keepdims=False)
    all_gates = lax.dynamic_slice_in_dim(all_gates, 2 * chip, 2, 2).astype(jnp.float32)
    here = jnp.array(place, jnp.int32)[chip]
    walk = jnp.array(cycle, jnp.int32)

    def gates_at(distance):
        return lax.dynamic_index_in_dim(
            all_gates, walk[(here + distance + chips_n) % chips_n], 0, keepdims=False
        )

    from_left, from_right = {0: tokens}, {0: tokens}
    for s in range(1, far):
        from_left[s] = send(from_left[s - 1], right)
        from_right[s] = send(from_right[s - 1], left)
    far_block = jnp.concatenate(
        [send(from_left[far - 1][:cut], right), send(from_right[far - 1][cut:], left)]
    )

    def outputs(blocks, distances):
        x = jnp.concatenate(blocks) if len(blocks) > 1 else blocks[0]
        g = jnp.concatenate([gates_at(d) for d in distances])
        return ffn(x, g, own, other)

    near = outputs([from_left[1], from_right[1], tokens], [-1, 1, 0])
    for_left, for_right = {1: near[:rows]}, {1: near[rows : 2 * rows]}
    mine = near[2 * rows :]
    for s in range(2, far):
        both = outputs([from_left[s], from_right[s]], [-s, s])
        for_left[s], for_right[s] = both[:rows], both[rows:]
    last = outputs([far_block], [far])

    to_right = send(last[:cut].astype(jnp.bfloat16), right)
    to_left = send(last[cut:].astype(jnp.bfloat16), left)
    to_right = jnp.pad(to_right, ((0, cut), (0, 0)))
    to_left = jnp.pad(to_left, ((cut, 0), (0, 0)))
    for s in range(far - 1, 0, -1):
        to_right = send((to_right.astype(jnp.float32) + for_right[s]).astype(jnp.bfloat16), right)
        to_left = send((to_left.astype(jnp.float32) + for_left[s]).astype(jnp.bfloat16), left)
    total = mine + to_right.astype(jnp.float32) + to_left.astype(jnp.float32)
    return total.astype(jnp.bfloat16)


def solution(mesh):
    cycle = chip_cycle(mesh.shape["expert"] // 2, mesh.shape["dp"])
    return jax.shard_map(
        functools.partial(on_device, cycle),
        mesh=mesh,
        in_specs=(
            P(("dp", "expert"), None),
            P(("dp", "expert"), None),
            P(("dp", "expert"), None),
            P("expert", None, None, None),
            P("expert", None, None, None),
            P("expert", None, None, None),
        ),
        out_specs=P(("dp", "expert"), None),
        check_vma=False,
    )
```

```python
import functools

import jax
import jax.numpy as jnp
from jax import lax
from jax.experimental import pallas as pl
from jax.experimental.pallas import tpu as pltpu
from jax.sharding import PartitionSpec as P


def chip_cycle(chips_n, rows_n):
    if rows_n % 2 or chips_n % rows_n or chips_n // rows_n < 2:
        return list(range(chips_n))
    deep = chips_n // rows_n
    walk = []
    for y in range(rows_n):
        zs = range(1, deep) if y % 2 == 0 else range(deep - 1, 0, -1)
        walk += [z * rows_n + y for z in zs]
    return walk + list(range(rows_n - 1, -1, -1))


def after(value, *earlier):
    def kernel(value_ref, *refs):
        refs[-1][...] = value_ref[...]

    return pl.pallas_call(
        kernel,
        out_shape=jax.ShapeDtypeStruct(value.shape, value.dtype),
        in_specs=[
            pl.BlockSpec(memory_space=pltpu.VMEM),
            *[pl.BlockSpec(memory_space=pl.ANY)] * len(earlier),
        ],
        out_specs=pl.BlockSpec(memory_space=pltpu.VMEM),
    )(value, *earlier)


def ffn_kernel(x_ref, gate_ref, g0, u0, d0, g1, u1, d1, earlier_ref, out_ref):
    i = pl.program_id(0)
    x = x_ref[...]
    expert = lax.axis_index("expert") // 2 * 2 + i % 2
    lanes = lax.broadcasted_iota(jnp.int32, gate_ref.shape, 1)
    gates = gate_ref[...].astype(jnp.float32)
    weight = jnp.sum(jnp.where(lanes == expert, gates, 0.0), axis=1, keepdims=True)

    def add(g_ref, u_ref, d_ref, first):
        gate_h = jnp.dot(x, g_ref[0], preferred_element_type=jnp.float32)
        up_h = jnp.dot(x, u_ref[0], preferred_element_type=jnp.float32)
        hidden = gate_h / (1.0 + jnp.exp(-gate_h)) * up_h
        hidden = hidden.astype(jnp.bfloat16)
        part = jnp.dot(hidden, d_ref[0], preferred_element_type=jnp.float32) * weight

        if first:

            @pl.when(i == 0)
            def _():
                out_ref[...] = part

            @pl.when(i > 0)
            def _():
                out_ref[...] += part

        else:
            out_ref[...] += part

    @pl.when(i < 2)
    def _():
        add(g0, u0, d0, True)

    @pl.when(i >= 2)
    def _():
        add(g1, u1, d1, False)


def ffn(x, gates, own, other, earlier):
    rows, width = x.shape
    half = own[0].shape[2]

    def early(shape):
        return pl.BlockSpec((1,) + shape, lambda i: (jnp.minimum(i, 1), 0, 0))

    def late(shape):
        return pl.BlockSpec((1,) + shape, lambda i: (jnp.maximum(i - 2, 0), 0, 0))

    flops = 4 * 2 * 3 * rows * width * half
    moved = 4 * 3 * width * half * 2 + rows * width * 6
    return pl.pallas_call(
        ffn_kernel,
        grid=(4,),
        out_shape=jax.ShapeDtypeStruct((rows, width), jnp.float32),
        in_specs=[
            pl.BlockSpec((rows, width), lambda i: (0, 0)),
            pl.BlockSpec((rows, gates.shape[1]), lambda i: (0, 0)),
            early((width, half)),
            early((width, half)),
            early((half, width)),
            late((width, half)),
            late((width, half)),
            late((half, width)),
            pl.BlockSpec(memory_space=pl.ANY),
        ],
        out_specs=pl.BlockSpec((rows, width), lambda i: (0, 0)),
        cost_estimate=pl.CostEstimate(
            flops=flops, bytes_accessed=moved, transcendentals=4 * rows * half
        ),
        compiler_params=pltpu.CompilerParams(vmem_limit_bytes=48 * 2**20),
    )(x, gates, *own, *other, earlier)


def on_device(cycle, tokens, expert_ids, route_weight, w_gate, w_up, w_down):
    devices_n = lax.axis_size("expert")
    chips_n = devices_n // 2
    rows = tokens.shape[0]
    cut = rows // 2
    far = chips_n // 2
    def turn(step):
        pairs = []
        for i, c in enumerate(cycle):
            to = cycle[(i + step) % chips_n]
            pairs += [(2 * c, 2 * to), (2 * c + 1, 2 * to + 1)]
        return pairs

    right, left = turn(1), turn(-1)
    swap = [(i, i ^ 1) for i in range(devices_n)]
    send = lambda value, pairs: lax.ppermute(value, "expert", pairs)

    gates = (route_weight / jnp.sum(route_weight, axis=1, keepdims=True)).astype(jnp.bfloat16)
    chosen = expert_ids[:, :, None] == jnp.arange(devices_n, dtype=jnp.int32)
    dense = jnp.sum(jnp.where(chosen, gates.astype(jnp.float32)[:, :, None], 0.0), axis=1)

    own = (w_gate[0], w_up[0], w_down[0])
    other = tuple(send(w, swap) for w in own)
    from_left, from_right = {0: tokens}, {0: tokens}
    for s in range(1, far):
        on_right, on_left = from_left[s - 1], from_right[s - 1]
        if s == min(3, far - 1):
            on_right, on_left = after(on_right, *other), after(on_left, *other)
        from_left[s] = send(on_right, right)
        from_right[s] = send(on_left, left)
    dense = dense.astype(jnp.bfloat16)
    sooner = after(dense, from_left[1])
    gates_at = {0: dense, -1: send(sooner, turn(1)), 1: send(sooner, turn(-1))}

    def outputs(blocks, distances, earlier):
        x = jnp.concatenate(blocks) if len(blocks) > 1 else blocks[0]
        g = jnp.concatenate([gates_at[d] for d in distances])
        return ffn(x, g, own, other, earlier)

    near = outputs([from_left[1], from_right[1]], [-1, 1], from_left[min(2, far - 1)])
    later = after(dense, near)
    for s in range(2, far):
        gates_at[-s], gates_at[s] = send(later, turn(s)), send(later, turn(-s))
    gates_at[far] = send(later, turn(far))
    far_block = jnp.concatenate(
        [
            send(after(from_left[far - 1][:cut], near), right),
            send(after(from_right[far - 1][cut:], near), left),
        ]
    )
    last = outputs([far_block], [far], near)
    for_left, for_right = {1: near[:rows]}, {1: near[rows:]}
    for s in range(2, far):
        both = outputs([from_left[s], from_right[s]], [-s, s], last)
        for_left[s], for_right[s] = both[:rows], both[rows:]

    to_right = send(last[:cut].astype(jnp.bfloat16), right)
    to_left = send(last[cut:].astype(jnp.bfloat16), left)
    to_right = jnp.pad(to_right, ((0, cut), (0, 0)))
    to_left = jnp.pad(to_left, ((cut, 0), (0, 0)))
    for s in range(far - 1, 0, -1):
        if s == 1:
            mine = outputs([tokens], [0], to_right)
        to_right = send((to_right.astype(jnp.float32) + for_right[s]).astype(jnp.bfloat16), right)
        to_left = send((to_left.astype(jnp.float32) + for_left[s]).astype(jnp.bfloat16), left)
    total = mine + to_right.astype(jnp.float32) + to_left.astype(jnp.float32)
    return total.astype(jnp.bfloat16)


def solution(mesh):
    cycle = chip_cycle(mesh.shape["expert"] // 2, mesh.shape["dp"])
    return jax.shard_map(
        functools.partial(on_device, cycle),
        mesh=mesh,
        in_specs=(
            P(("dp", "expert"), None),
            P(("dp", "expert"), None),
            P(("dp", "expert"), None),
            P("expert", None, None, None),
            P("expert", None, None, None),
            P("expert", None, None, None),
        ),
        out_specs=P(("dp", "expert"), None),
        check_vma=False,
    )
```

```python
import functools

import jax
import jax.numpy as jnp
from jax import lax
from jax.experimental import pallas as pl
from jax.experimental.pallas import tpu as pltpu
from jax.sharding import PartitionSpec as P


def chip_cycle(chips_n, rows_n):
    if rows_n % 2 or chips_n % rows_n or chips_n // rows_n < 2:
        return list(range(chips_n))
    deep = chips_n // rows_n
    walk = []
    for y in range(rows_n):
        zs = range(1, deep) if y % 2 == 0 else range(deep - 1, 0, -1)
        walk += [z * rows_n + y for z in zs]
    return walk + list(range(rows_n - 1, -1, -1))


def gates_kernel(chips_n, gate_ref, out_ref, send_sems, recv_sems):
    me = lax.axis_index("expert")
    chip, core = me // 2, me % 2
    peers = [{"expert": (chip + d) % chips_n * 2 + core} for d in range(1, chips_n)]
    barrier = pltpu.get_barrier_semaphore()
    for peer in peers:
        pl.semaphore_signal(barrier, inc=1, device_id=peer, device_id_type=pl.DeviceIdType.MESH)
    pl.semaphore_wait(barrier, chips_n - 1)
    copies = []
    for i, peer in enumerate(peers):
        copies.append(
            pltpu.make_async_remote_copy(
                src_ref=gate_ref,
                dst_ref=out_ref.at[i + 1],
                send_sem=send_sems.at[i],
                recv_sem=recv_sems.at[i],
                device_id=peer,
                device_id_type=pl.DeviceIdType.MESH,
            )
        )
        copies[i].start()
    out_ref[0] = gate_ref[...]
    for copy in copies:
        copy.wait()


def share_gates(dense, chips_n):
    return pl.pallas_call(
        functools.partial(gates_kernel, chips_n),
        out_shape=jax.ShapeDtypeStruct((chips_n,) + dense.shape, dense.dtype),
        in_specs=[pl.BlockSpec(memory_space=pltpu.VMEM)],
        out_specs=pl.BlockSpec(memory_space=pltpu.VMEM),
        scratch_shapes=[pltpu.SemaphoreType.DMA((chips_n - 1,))] * 2,
        compiler_params=pltpu.CompilerParams(collective_id=0, has_side_effects=True),
    )(dense)


def ffn_kernel(cycle, distances, x_ref, gate_ref, g0, u0, d0, g1, u1, d1, earlier_ref, out_ref):
    i = pl.program_id(0)
    x = x_ref[...]
    chips_n = len(cycle)
    chip = lax.axis_index("expert") // 2
    place = sum(jnp.where(chip == c, p, 0) for p, c in enumerate(cycle))
    lanes = lax.broadcasted_iota(jnp.int32, gate_ref.shape[1:], 1)
    weights = []
    for distance in distances:
        there = (place + distance + chips_n) % chips_n
        source = sum(jnp.where(there == p, c, 0) for p, c in enumerate(cycle))
        gates = gate_ref[(chip - source + chips_n) % chips_n].astype(jnp.float32)
        picked = jnp.where(lanes == chip * 2 + i % 2, gates, 0.0)
        weights.append(jnp.sum(picked, axis=1, keepdims=True))
    weight = jnp.concatenate(weights)

    def add(g_ref, u_ref, d_ref, first):
        gate_h = jnp.dot(x, g_ref[0], preferred_element_type=jnp.float32)
        up_h = jnp.dot(x, u_ref[0], preferred_element_type=jnp.float32)
        hidden = gate_h / (1.0 + jnp.exp(-gate_h)) * up_h
        hidden = hidden.astype(jnp.bfloat16)
        part = jnp.dot(hidden, d_ref[0], preferred_element_type=jnp.float32) * weight

        if first:

            @pl.when(i == 0)
            def _():
                out_ref[...] = part

            @pl.when(i > 0)
            def _():
                out_ref[...] += part

        else:
            out_ref[...] += part

    @pl.when(i < 2)
    def _():
        add(g0, u0, d0, True)

    @pl.when(i >= 2)
    def _():
        add(g1, u1, d1, False)


def ffn(cycle, distances, x, gates, own, other, earlier):
    rows, width = x.shape
    half = own[0].shape[2]

    def early(shape):
        return pl.BlockSpec((1,) + shape, lambda i: (jnp.minimum(i, 1), 0, 0))

    def late(shape):
        return pl.BlockSpec((1,) + shape, lambda i: (jnp.maximum(i - 2, 0), 0, 0))

    flops = 4 * 2 * 3 * rows * width * half
    moved = 4 * 3 * width * half * 2 + rows * width * 6
    return pl.pallas_call(
        functools.partial(ffn_kernel, cycle, distances),
        grid=(4,),
        out_shape=jax.ShapeDtypeStruct((rows, width), jnp.float32),
        in_specs=[
            pl.BlockSpec((rows, width), lambda i: (0, 0)),
            pl.BlockSpec(gates.shape, lambda i: (0, 0, 0)),
            early((width, half)),
            early((width, half)),
            early((half, width)),
            late((width, half)),
            late((width, half)),
            late((half, width)),
            pl.BlockSpec(memory_space=pl.ANY),
        ],
        out_specs=pl.BlockSpec((rows, width), lambda i: (0, 0)),
        cost_estimate=pl.CostEstimate(
            flops=flops, bytes_accessed=moved, transcendentals=4 * rows * half
        ),
        compiler_params=pltpu.CompilerParams(vmem_limit_bytes=48 * 2**20),
    )(x, gates, *own, *other, earlier)


def on_device(cycle, tokens, expert_ids, route_weight, w_gate, w_up, w_down):
    devices_n = lax.axis_size("expert")
    chips_n = devices_n // 2
    rows = tokens.shape[0]
    cut = rows // 2
    far = chips_n // 2
    def turn(step):
        pairs = []
        for i, c in enumerate(cycle):
            to = cycle[(i + step) % chips_n]
            pairs += [(2 * c, 2 * to), (2 * c + 1, 2 * to + 1)]
        return pairs

    right, left = turn(1), turn(-1)
    swap = [(i, i ^ 1) for i in range(devices_n)]
    send = lambda value, pairs: lax.ppermute(value, "expert", pairs)

    gates = (route_weight / jnp.sum(route_weight, axis=1, keepdims=True)).astype(jnp.bfloat16)
    lanes = -(-devices_n // 128) * 128
    chosen = expert_ids[:, :, None] == jnp.arange(lanes, dtype=jnp.int32)
    dense = jnp.sum(jnp.where(chosen, gates.astype(jnp.float32)[:, :, None], 0.0), axis=1)

    own = (w_gate[0], w_up[0], w_down[0])
    other = tuple(send(w, swap) for w in own)
    from_left, from_right = {0: tokens}, {0: tokens}
    for s in range(1, far):
        from_left[s] = send(from_left[s - 1], right)
        from_right[s] = send(from_right[s - 1], left)
    far_block = jnp.concatenate(
        [send(from_left[far - 1][:cut], right), send(from_right[far - 1][cut:], left)]
    )
    all_gates = share_gates(dense.astype(jnp.bfloat16), chips_n)

    def outputs(blocks, distances, earlier):
        x = jnp.concatenate(blocks) if len(blocks) > 1 else blocks[0]
        return ffn(cycle, distances, x, all_gates, own, other, earlier)

    last = outputs([far_block], [far], far_block)
    for_left, for_right = {}, {}
    for s in range(1, far):
        both = outputs([from_left[s], from_right[s]], [-s, s], last)
        for_left[s], for_right[s] = both[:rows], both[rows:]

    to_right = send(last[:cut].astype(jnp.bfloat16), right)
    to_left = send(last[cut:].astype(jnp.bfloat16), left)
    to_right = jnp.pad(to_right, ((0, cut), (0, 0)))
    to_left = jnp.pad(to_left, ((cut, 0), (0, 0)))
    for s in range(far - 1, 0, -1):
        if s == 1:
            mine = outputs([tokens], [0], to_right)
        to_right = send((to_right.astype(jnp.float32) + for_right[s]).astype(jnp.bfloat16), right)
        to_left = send((to_left.astype(jnp.float32) + for_left[s]).astype(jnp.bfloat16), left)
    total = mine + to_right.astype(jnp.float32) + to_left.astype(jnp.float32)
    return total.astype(jnp.bfloat16)


def solution(mesh):
    cycle = chip_cycle(mesh.shape["expert"] // 2, mesh.shape["dp"])
    return jax.shard_map(
        functools.partial(on_device, cycle),
        mesh=mesh,
        in_specs=(
            P(("dp", "expert"), None),
            P(("dp", "expert"), None),
            P(("dp", "expert"), None),
            P("expert", None, None, None),
            P("expert", None, None, None),
            P("expert", None, None, None),
        ),
        out_specs=P(("dp", "expert"), None),
        check_vma=False,
    )
```

```python
import functools

import jax
import jax.numpy as jnp
from jax import lax
from jax.experimental import pallas as pl
from jax.experimental.pallas import tpu as pltpu
from jax.sharding import PartitionSpec as P


def chip_cycle(chips_n, rows_n):
    if rows_n % 2 or chips_n % rows_n or chips_n // rows_n < 2:
        return list(range(chips_n))
    deep = chips_n // rows_n
    walk = []
    for y in range(rows_n):
        zs = range(1, deep) if y % 2 == 0 else range(deep - 1, 0, -1)
        walk += [z * rows_n + y for z in zs]
    return walk + list(range(rows_n - 1, -1, -1))


def gates_kernel(chips_n, gate_ref, out_ref, send_sems, recv_sems):
    me = lax.axis_index("expert")
    chip, core = me // 2, me % 2
    peers = [{"expert": (chip + d) % chips_n * 2 + core} for d in range(1, chips_n)]
    barrier = pltpu.get_barrier_semaphore()
    for peer in peers:
        pl.semaphore_signal(barrier, inc=1, device_id=peer, device_id_type=pl.DeviceIdType.MESH)
    pl.semaphore_wait(barrier, chips_n - 1)
    copies = []
    for i, peer in enumerate(peers):
        copies.append(
            pltpu.make_async_remote_copy(
                src_ref=gate_ref,
                dst_ref=out_ref.at[i + 1],
                send_sem=send_sems.at[i],
                recv_sem=recv_sems.at[i],
                device_id=peer,
                device_id_type=pl.DeviceIdType.MESH,
            )
        )
        copies[i].start()
    out_ref[0] = gate_ref[...]
    for copy in copies:
        copy.wait()


def share_gates(dense, chips_n):
    return pl.pallas_call(
        functools.partial(gates_kernel, chips_n),
        out_shape=jax.ShapeDtypeStruct((chips_n,) + dense.shape, dense.dtype),
        in_specs=[pl.BlockSpec(memory_space=pltpu.VMEM)],
        out_specs=pl.BlockSpec(memory_space=pltpu.VMEM),
        scratch_shapes=[pltpu.SemaphoreType.DMA((chips_n - 1,))] * 2,
        compiler_params=pltpu.CompilerParams(collective_id=0, has_side_effects=True),
    )(dense)


def halves_kernel(first_ref, second_ref, earlier_ref, top_ref, bottom_ref):
    cut = top_ref.shape[0]
    top_ref[...] = first_ref[:cut]
    bottom_ref[...] = second_ref[cut:]


def halves(first, second, earlier):
    half = jax.ShapeDtypeStruct((first.shape[0] // 2, first.shape[1]), first.dtype)
    vmem = pl.BlockSpec(memory_space=pltpu.VMEM)
    return pl.pallas_call(
        halves_kernel,
        out_shape=(half, half),
        in_specs=[vmem, vmem, pl.BlockSpec(memory_space=pl.ANY)],
        out_specs=(vmem, vmem),
    )(first, second, earlier)


def ffn_kernel(cycle, distances, blocks_n, *refs):
    x_refs, refs = refs[:blocks_n], refs[blocks_n:]
    gate_ref, own, other = refs[0], refs[1:4], refs[4:7]
    out_ref, x_ref, held, sems = refs[8], refs[9], refs[10:13], refs[13]
    copies = []
    for i in range(4):
        slab = own if i < 2 else other
        row = [
            pltpu.make_async_copy(slab[k].at[i % 2], held[k].at[i], sems.at[i, k]) for k in range(3)
        ]
        for copy in row:
            copy.start()
        copies.append(row)

    first = 0
    for ref in x_refs:
        x_ref[first : first + ref.shape[0]] = ref[...]
        first += ref.shape[0]

    chips_n = len(cycle)
    chip = lax.axis_index("expert") // 2
    place = sum(jnp.where(chip == c, p, 0) for p, c in enumerate(cycle))
    lanes = lax.broadcasted_iota(jnp.int32, gate_ref.shape[1:], 1)
    weights = [[], []]
    for distance in distances:
        there = (place + distance + chips_n) % chips_n
        source = sum(jnp.where(there == p, c, 0) for p, c in enumerate(cycle))
        gates = gate_ref[(chip - source + chips_n) % chips_n].astype(jnp.float32)
        for j in range(2):
            picked = jnp.where(lanes == chip * 2 + j, gates, 0.0)
            weights[j].append(jnp.sum(picked, axis=1, keepdims=True))
    weights = [jnp.concatenate(w) for w in weights]

    x = x_ref[...]
    for i in range(4):
        copies[i][0].wait()
        gate_h = jnp.dot(x, held[0][i], preferred_element_type=jnp.float32)
        copies[i][1].wait()
        up_h = jnp.dot(x, held[1][i], preferred_element_type=jnp.float32)
        hidden = gate_h / (1.0 + jnp.exp(-gate_h)) * up_h * weights[i % 2]
        copies[i][2].wait()
        part = jnp.dot(hidden.astype(jnp.bfloat16), held[2][i], preferred_element_type=jnp.float32)
        if i == 0:
            out_ref[...] = part
        else:
            out_ref[...] += part


def ffn(cycle, distances, blocks, gates, own, other, earlier):
    rows, width = sum(b.shape[0] for b in blocks), blocks[0].shape[1]
    half = own[0].shape[2]
    vmem, anywhere = pl.BlockSpec(memory_space=pltpu.VMEM), pl.BlockSpec(memory_space=pl.ANY)
    return pl.pallas_call(
        functools.partial(ffn_kernel, cycle, distances, len(blocks)),
        out_shape=jax.ShapeDtypeStruct((rows, width), jnp.float32),
        in_specs=[vmem] * len(blocks) + [vmem] + [anywhere] * 7,
        out_specs=vmem,
        scratch_shapes=[
            pltpu.VMEM((rows, width), jnp.bfloat16),
            pltpu.VMEM((4, width, half), jnp.bfloat16),
            pltpu.VMEM((4, width, half), jnp.bfloat16),
            pltpu.VMEM((4, half, width), jnp.bfloat16),
            pltpu.SemaphoreType.DMA((4, 3)),
        ],
        cost_estimate=pl.CostEstimate(
            flops=4 * 2 * 3 * rows * width * half,
            bytes_accessed=4 * 3 * width * half * 2 + rows * width * 6,
            transcendentals=4 * rows * half,
        ),
        compiler_params=pltpu.CompilerParams(vmem_limit_bytes=48 * 2**20),
    )(*blocks, gates, *own, *other, earlier)


def on_device(cycle, tokens, expert_ids, route_weight, w_gate, w_up, w_down):
    devices_n = lax.axis_size("expert")
    chips_n = devices_n // 2
    rows = tokens.shape[0]
    cut = rows // 2
    far = chips_n // 2
    def turn(step):
        pairs = []
        for i, c in enumerate(cycle):
            to = cycle[(i + step) % chips_n]
            pairs += [(2 * c, 2 * to), (2 * c + 1, 2 * to + 1)]
        return pairs

    right, left = turn(1), turn(-1)
    swap = [(i, i ^ 1) for i in range(devices_n)]
    send = lambda value, pairs: lax.ppermute(value, "expert", pairs)

    gates = (route_weight / jnp.sum(route_weight, axis=1, keepdims=True)).astype(jnp.bfloat16)
    lanes = -(-devices_n // 128) * 128
    chosen = expert_ids[:, :, None] == jnp.arange(lanes, dtype=jnp.int32)
    dense = jnp.sum(jnp.where(chosen, gates.astype(jnp.float32)[:, :, None], 0.0), axis=1)

    own = (w_gate[0], w_up[0], w_down[0])
    other = tuple(send(w, swap) for w in own)
    from_left, from_right = {0: tokens}, {0: tokens}
    for s in range(1, far):
        from_left[s] = send(from_left[s - 1], right)
        from_right[s] = send(from_right[s - 1], left)
    all_gates = share_gates(dense.astype(jnp.bfloat16), chips_n)
    top, bottom = halves(from_left[far - 1], from_right[far - 1], all_gates)
    top, bottom = send(top, right), send(bottom, left)

    def outputs(blocks, distances, earlier):
        return ffn(cycle, distances, blocks, all_gates, own, other, earlier)

    last = outputs([top, bottom], [far], top)
    for_left, for_right = {}, {}
    for s in range(1, far):
        both = outputs([from_left[s], from_right[s]], [-s, s], last)
        for_left[s], for_right[s] = both[:rows], both[rows:]

    to_right = send(last[:cut].astype(jnp.bfloat16), right)
    to_left = send(last[cut:].astype(jnp.bfloat16), left)
    to_right = jnp.pad(to_right, ((0, cut), (0, 0)))
    to_left = jnp.pad(to_left, ((cut, 0), (0, 0)))
    for s in range(far - 1, 0, -1):
        if s == 1:
            mine = outputs([tokens], [0], to_right)
        to_right = send((to_right.astype(jnp.float32) + for_right[s]).astype(jnp.bfloat16), right)
        to_left = send((to_left.astype(jnp.float32) + for_left[s]).astype(jnp.bfloat16), left)
    total = mine + to_right.astype(jnp.float32) + to_left.astype(jnp.float32)
    return total.astype(jnp.bfloat16)


def solution(mesh):
    cycle = chip_cycle(mesh.shape["expert"] // 2, mesh.shape["dp"])
    return jax.shard_map(
        functools.partial(on_device, cycle),
        mesh=mesh,
        in_specs=(
            P(("dp", "expert"), None),
            P(("dp", "expert"), None),
            P(("dp", "expert"), None),
            P("expert", None, None, None),
            P("expert", None, None, None),
            P("expert", None, None, None),
        ),
        out_specs=P(("dp", "expert"), None),
        check_vma=False,
    )
```
